512 devices in a mesh: pipe: 16 (over z), blk: 32 (over x, y, core).
Axes of the slice: x: 4, y: 4, z: 16, core: 2. Of those that a mesh axis runs over, the one named last changes fastest.
Arguments:
- stream: bfloat16 [16, 128, 6144], P('pipe', 'blk'), may hold values from -6 to 6
- arrivals: bfloat16 [3, 128, 6144], P(None, 'blk'), may hold values from -6 to 6
- ln_gain: bfloat16 [16, 6144], P('pipe'), may hold values from 0.099609375 to 1.8984375
- ln_bias: bfloat16 [16, 6144], P('pipe'), may hold values from -3 to 3
- up_weight: bfloat16 [16, 6144, 4096], P('pipe', None, 'blk'), may hold values from -0.078125 to 0.078125
- up_bias: bfloat16 [16, 4096], P('pipe', 'blk'), may hold values from -3 to 3
- down_weight: bfloat16 [16, 4096, 6144], P('pipe', 'blk'), may hold values from -0.1875 to 0.1875
- down_bias: bfloat16 [16, 6144], P('pipe'), may hold values from -3 to 3
- active: int32 [4, 16, 2, 16], P(None, 'pipe'), may hold values from -1 to 31, as said below
Outputs:
- passed: bfloat16 [16, 4, 128, 6144], P('pipe', None, 'blk')
The draws below stay inside these ranges and needn't reach their ends.
Inputs may be any that keep to these rules, and one draw needn't show every extreme that they name: Each list holds between 8 and 16 distinct block ids, followed by -1 padding; some blocks are active far more often than others.
All inputs are finite; a program needn't handle non-finite values.
Results may differ from the reference program's by a relative error of at most 0.019.
Values may be sent and summed in bfloat16 or wider, within the bound.
No kernel may reach another device: no remote copies, remote signals or barrier semaphores. Data moves between devices by JAX's collectives and lax.ppermute only.
A program may use at most 64 MiB of HBM per device.

```python
import jax
import jax.numpy as jnp
from jax import lax

D = 6144
BLOCK = 128
TILE = 64
TILES = 2
TICKS = 4
NBLK = 32
KMAX = 16
ROWS = 128
N_PIPE = 16
N_BLK = 32


def draw_active(key, part):
    key_pop = jax.random.fold_in(key, 11)
    key_score = jax.random.fold_in(key, 12)
    key_count = jax.random.fold_in(key, 13)
    popular = (jax.random.permutation(key_pop, N_BLK) < N_BLK // 4).astype(jnp.int32)
    weight_int = 1 + 3 * popular
    scores = jax.random.randint(key_score, (TICKS, N_PIPE, TILES, N_BLK), 0, 65536, dtype=jnp.int32)
    scores = scores * weight_int * N_BLK + jnp.arange(N_BLK, dtype=jnp.int32)
    chosen = lax.top_k(scores, KMAX)[1].astype(jnp.int32)
    counts = jax.random.randint(key_count, (TICKS, N_PIPE, TILES, 1), KMAX // 2, KMAX + 1, dtype=jnp.int32)
    slots = jnp.arange(KMAX, dtype=jnp.int32)
    return jnp.where(slots < counts, chosen, -1).astype(jnp.int32)


def block_levels(key, shape, pieces, low, high):
    level, own = 1.0, jax.random.fold_in(key, 6)
    for dim, parts in pieces:
        draws = jnp.exp(jax.random.uniform(jax.random.fold_in(own, dim), (parts,), jnp.float32, low / len(pieces), high / len(pieces)))
        level = level * jnp.repeat(draws, shape[dim] // parts).reshape([-1 if axis == dim else 1 for axis in range(len(shape))])
    return level


def normal_values(own_key, dims, width, reach, pieces=(), kind=jnp.bfloat16):
    loudness = block_levels(own_key, dims, pieces, -0.22, 0.18) if pieces else 1.0
    entries = jax.random.normal(own_key, dims, jnp.float32) * width * loudness
    return jnp.minimum(jnp.maximum(entries, -reach), reach).astype(kind)


def setup_inputs(seed: int = 0) -> dict:
    key_list = jax.random.split(jax.random.key(seed), 10)
    stream = normal_values(key_list[0], (N_PIPE, ROWS, D), 1.0, 6.0, ((0, 16), (1, 32)))
    arrivals = normal_values(key_list[1], (TICKS - 1, ROWS, D), 1.0, 6.0, ((1, 32),))
    ln_gain = jnp.clip(1.0 + 0.18 * jax.random.normal(key_list[2], (N_PIPE, D), jnp.float32), 0.099609375, 1.8984375).astype(jnp.bfloat16)
    ln_bias = normal_values(key_list[3], (N_PIPE, D), 0.5, 3.0, ((0, 16),))
    up_weight = normal_values(key_list[4], (N_PIPE, D, NBLK * BLOCK), D ** -0.5, 0.078125, ((0, 16), (2, 32)))
    up_bias = normal_values(key_list[5], (N_PIPE, NBLK * BLOCK), 0.5, 3.0, ((0, 16), (1, 32)))
    down_weight = normal_values(key_list[6], (N_PIPE, NBLK * BLOCK, D), (KMAX * BLOCK // 2) ** -0.5, 0.1875, ((0, 16), (1, 32)))
    down_bias = normal_values(key_list[7], (N_PIPE, D), 0.5, 3.0, ((0, 16),))
    active = draw_active(jax.random.fold_in(key_list[9], 71), 0)
    return {"stream": stream, "arrivals": arrivals, "ln_gain": ln_gain, "ln_bias": ln_bias, "up_weight": up_weight, "up_bias": up_bias, "down_weight": down_weight, "down_bias": down_bias, "active": active}


def layer_norm(rows, gain_row, shift_row):
    widened = rows.astype(jnp.float32)
    row_mean = lax.optimization_barrier(jnp.mean(widened, axis=-1, keepdims=True))
    centred = widened - row_mean
    row_var = lax.optimization_barrier(jnp.mean(centred * centred, axis=-1, keepdims=True))
    scaled = centred * lax.rsqrt(row_var + 1e-05)
    return (scaled * gain_row.astype(jnp.float32) + shift_row.astype(jnp.float32)).astype(jnp.bfloat16)

def section_layer(rows, tile_lists, gain_row, shift_row, w_up, b_up, w_down, b_down):
    normed = layer_norm(rows, gain_row, shift_row)
    up_blocks = w_up.reshape(D, NBLK, BLOCK)
    bias_blocks = b_up.reshape(NBLK, BLOCK)
    down_blocks = w_down.reshape(NBLK, BLOCK, D)
    sums = []
    for tile_index in range(TILES):
        block_ids = tile_lists[tile_index]
        valid = (block_ids >= 0).astype(jnp.float32)
        safe_ids = jnp.maximum(block_ids, 0).astype(jnp.int32)
        chosen_up = jnp.take(up_blocks, safe_ids, axis=1).astype(jnp.float32)
        chosen_bias = jnp.take(bias_blocks, safe_ids, axis=0).astype(jnp.float32)
        chosen_down = jnp.take(down_blocks, safe_ids, axis=0).astype(jnp.float32)
        segment = normed[tile_index * TILE:(tile_index + 1) * TILE].astype(jnp.float32)
        preact = jnp.einsum('rd,dkb->rkb', segment, chosen_up) + chosen_bias[None]
        activity = (jnp.maximum(preact, 0.0) * valid[None, :, None]).astype(jnp.bfloat16)
        partials = jnp.einsum('rkb,kbd->krd', activity.astype(jnp.float32), chosen_down).astype(jnp.bfloat16)
        sums.append(lax.optimization_barrier(jnp.sum(partials.astype(jnp.float32), axis=0)))
    summed = jnp.concatenate(sums, axis=0)
    return (rows.astype(jnp.float32) + summed + b_down.astype(jnp.float32)).astype(jnp.bfloat16)

def reference(stream, arrivals, ln_gain, ln_bias, up_weight, up_bias, down_weight, down_bias, active):
    current = [stream[section] for section in range(N_PIPE)]
    per_section = [[] for section in range(N_PIPE)]
    for step_index in range(TICKS):
        produced = []
        for section in range(N_PIPE):
            output_rows = section_layer(current[section], active[step_index, section], ln_gain[section], ln_bias[section], up_weight[section], up_bias[section], down_weight[section], down_bias[section])
            produced.append(output_rows)
            per_section[section].append(output_rows)
        if step_index + 1 < TICKS:
            current = [arrivals[step_index]] + produced[:-1]
    return jnp.stack([jnp.stack(per_section[section]) for section in range(N_PIPE)])
```

```python
import functools

import jax
import jax.numpy as jnp
from jax import lax
from jax.experimental import pallas as pl
from jax.experimental.pallas import tpu as pltpu
from jax.sharding import PartitionSpec as P

F32, BF16 = jnp.float32, jnp.bfloat16
TILE = 64
TICKS = 4
CHIPS = 16
EPS = 1e-05
SIDE = 128

VMEM = pl.BlockSpec(memory_space=pltpu.VMEM)
SMEM = pl.BlockSpec(memory_space=pltpu.SMEM)
PARAMS = pltpu.CompilerParams(vmem_limit_bytes=40 * 1024 * 1024)


def half_of(c, half):
    return pl.ds(pl.multiple_of(c * half, 128), half)


def split_kernel(stream_ref, arrivals_ref, keep_ref, send_ref):
    c = lax.axis_index("blk") % 2
    half = keep_ref.shape[2]
    keep_ref[0] = stream_ref[0, :, half_of(c, half)]
    send_ref[0] = stream_ref[0, :, half_of(1 - c, half)]
    keep_ref[1:] = arrivals_ref[:, :, half_of(c, half)]
    send_ref[1:] = arrivals_ref[:, :, half_of(1 - c, half)]


def weights_kernel(up_ref, up_far_ref, down_ref, down_far_ref, gain_ref, bias_ref, up_bias_ref, up_out, down_out, rows_out):
    c = lax.axis_index("blk") % 2
    half = up_far_ref.shape[0]
    block = up_far_ref.shape[1]
    up_out[:, :block] = up_ref[0, pl.ds(pl.multiple_of(c * half, 128), half), :]
    up_out[:, block:] = up_far_ref[...]
    down_out[:block] = down_ref[0, :, half_of(c, half)]
    down_out[block:] = down_far_ref[...]
    gain = gain_ref[:, half_of(c, half)].astype(F32)
    bias = bias_ref[:, half_of(c, half)].astype(F32)
    row = lax.broadcasted_iota(jnp.int32, (8, half), 0)
    both = jnp.where(row == 0, gain, jnp.where(row == 1, bias, 0.0)).astype(BF16)
    sums = jnp.dot(both, up_out[...], preferred_element_type=F32)
    row = lax.broadcasted_iota(jnp.int32, (8, block), 0)
    own = jnp.where(row == 1, up_bias_ref[...].astype(F32), 0.0)
    rows_out[:, :block] = sums[:, :block] + own
    rows_out[:, block:] = sums[:, block:]


def norm_kernel(step, moved_ref, keep_ref, far_ref, gain_ref, rows_out, send_out, scratch):
    c = lax.axis_index("blk") % 2
    half = rows_out.shape[1]

    def local():
        near, far = keep_ref[step].astype(F32), far_ref[step].astype(F32)

        @pl.when(c == 0)
        def _():
            scratch[0:4] = near
            scratch[4:8] = far

        @pl.when(c == 1)
        def _():
            scratch[0:4] = far
            scratch[4:8] = near

    if step == 0:
        local()
    else:
        first = lax.axis_index("pipe") == 0
        pl.when(first)(local)

        @pl.when(jnp.logical_not(first))
        def _():
            scratch[...] = moved_ref[...].astype(F32)

    rows = scratch[...]
    rows_out[...] = rows.astype(BF16)
    mean = jnp.mean(rows, axis=1, keepdims=True)
    centred = rows - mean
    square = jnp.sum(centred * centred, axis=1, keepdims=True)
    scaled = (centred * gain_ref[:, half_of(c, half)].astype(F32)).astype(BF16)
    lane = lax.broadcasted_iota(jnp.int32, (8, SIDE), 1)
    side = jnp.zeros((8, SIDE), F32)
    for base, value in ((0, mean), (3, square)):
        for piece in range(3):
            part = value.astype(BF16).astype(F32)
            side = jnp.where(lane == base + piece, part, side)
            value = value - part
    side = side.astype(BF16)
    for chip in range(send_out.shape[0]):
        send_out[chip, :, :half] = scaled
        send_out[chip, :, half:] = side


def up_kernel(gathered_ref, up_ref, rows_ref, out_ref):
    half, wide = up_ref.shape
    count = gathered_ref.shape[0]
    out_ref[:count, :wide] = jnp.dot(gathered_ref[:, :half], up_ref[...], preferred_element_type=F32)
    out_ref[:count, wide:] = gathered_ref[:, half:].astype(F32)
    out_ref[count:, :wide] = rows_ref[...]
    out_ref[count:, wide:] = jnp.zeros((8, SIDE), F32)


def down_kernel(step, near_ref, far_ref, active_ref, down_ref, out_ref):
    wide, half = down_ref.shape
    block = wide // 2
    count = out_ref.shape[0]
    j = lax.axis_index("blk")
    near_side, far_side = near_ref[:count, wide:], far_ref[:count, wide:]
    lane = lax.broadcasted_iota(jnp.int32, (count, SIDE), 1)
    apart = jnp.sum(jnp.where(lane < 3, near_side - far_side, 0.0), axis=1, keepdims=True) * 0.5
    square = jnp.sum(jnp.where((lane >= 3) & (lane < 6), near_side + far_side, 0.0), axis=1, keepdims=True)
    scale = lax.rsqrt(square / (2 * half) + apart * apart + EPS)
    tile = lax.broadcasted_iota(jnp.int32, (count, block), 0) // TILE
    acts = []
    for mine, other, owner in (((0, block), (block, wide), j), ((block, wide), (0, block), j + 1 - 2 * (j % 2))):
        near = near_ref[:count, mine[0] : mine[1]]
        far = far_ref[:count, other[0] : other[1]]
        gain_sum = near_ref[count : count + 1, mine[0] : mine[1]] - far_ref[count : count + 1, other[0] : other[1]]
        bias_sum = near_ref[count + 1 : count + 2, mine[0] : mine[1]] + far_ref[count + 1 : count + 2, other[0] : other[1]]
        flag = jnp.zeros((count, block), F32)
        for t in range(active_ref.shape[2]):
            found = jnp.int32(0)
            for k in range(active_ref.shape[3]):
                found = found | (active_ref[step, 0, t, k] == owner).astype(jnp.int32)
            flag = jnp.where(tile == t, found.astype(F32), flag)
        preact = scale * (near + far + apart * gain_sum) + bias_sum
        acts.append((jnp.maximum(preact, 0.0) * flag).astype(BF16))
    acts = jnp.concatenate(acts, axis=1)
    chunk = 512
    for at in range(0, half, chunk):
        out_ref[:, at : at + chunk] = jnp.dot(acts, down_ref[:, at : at + chunk], preferred_element_type=F32).astype(BF16)


def sum_kernel(parts_ref, rows_ref, bias_ref, out_ref):
    c = lax.axis_index("blk") % 2
    half = out_ref.shape[1]
    total = rows_ref[...].astype(F32) + bias_ref[:, half_of(c, half)].astype(F32)
    for chip in range(parts_ref.shape[0]):
        total += parts_ref[chip].astype(F32)
    out_ref[...] = total.astype(BF16)


def final_kernel(produced_refs, far_ref, out_ref):
    c = lax.axis_index("blk") % 2
    half = far_ref.shape[2]

    def at(core):
        for step, ref in enumerate(produced_refs):
            rows = ref[...].astype(F32)
            out_ref[0, step, :, core * half : (core + 1) * half] = rows[core * 4 : core * 4 + 4].astype(BF16)
        out_ref[0, :, :, (1 - core) * half : (2 - core) * half] = far_ref[...]

    pl.when(c == 0)(functools.partial(at, 0))
    pl.when(c == 1)(functools.partial(at, 1))


def gather_far_kernel(produced_refs, out_ref):
    c = lax.axis_index("blk") % 2

    def at(core):
        for step, ref in enumerate(produced_refs):
            rows = ref[...].astype(F32)
            out_ref[step] = rows[(1 - core) * 4 : (1 - core) * 4 + 4].astype(BF16)

    pl.when(c == 0)(functools.partial(at, 0))
    pl.when(c == 1)(functools.partial(at, 1))


def call(kernel, outs, *args, specs=None, scratch=()):
    single = isinstance(outs, jax.ShapeDtypeStruct)
    return pl.pallas_call(
        kernel,
        out_shape=outs,
        in_specs=list(specs) if specs else [VMEM] * len(args),
        out_specs=VMEM if single else [VMEM] * len(outs),
        scratch_shapes=list(scratch),
        compiler_params=PARAMS,
    )(*args)


def on_device(stream, arrivals, ln_gain, ln_bias, up_weight, up_bias, down_weight, down_bias, active):
    shape = jax.ShapeDtypeStruct
    blocks = lax.axis_size("blk")
    pipes = lax.axis_size("pipe")
    rows_dev, width = stream.shape[1], stream.shape[2]
    block = up_weight.shape[2]
    half = width // 2
    rows_chip = 2 * rows_dev
    rows_all = rows_chip * CHIPS
    c = lax.axis_index("blk") % 2
    same_core = [[2 * chip + core for chip in range(CHIPS)] for core in range(2)]

    def swap(x):
        return lax.ppermute(x, "blk", [(i, i ^ 1) for i in range(blocks)])

    def trade(x):
        return lax.all_to_all(x, "blk", 0, 0, axis_index_groups=same_core, tiled=True)

    keep, send = call(split_kernel, [shape((TICKS, rows_dev, half), BF16)] * 2, stream, arrivals)
    far = swap(send)
    up_far = swap(lax.dynamic_slice(up_weight[0], ((1 - c) * half, 0), (half, block)))
    down_far = swap(lax.dynamic_slice(down_weight[0], (0, (1 - c) * half), (block, half)))
    up_pair, down_pair, bias_rows = call(
        weights_kernel,
        [shape((half, 2 * block), BF16), shape((2 * block, half), BF16), shape((8, 2 * block), F32)],
        up_weight, up_far, down_weight, down_far, ln_gain, ln_bias, up_bias,
    )
    moved = None
    produced = []
    for step in range(TICKS):
        args = [keep, far, ln_gain] if step == 0 else [moved, keep, far, ln_gain]
        kernel = functools.partial(norm_kernel, step) if step else (lambda *refs: norm_kernel(0, None, *refs))
        rows, outgoing = call(
            kernel,
            [shape((rows_chip, half), BF16), shape((CHIPS, rows_chip, half + SIDE), BF16)],
            *args,
            scratch=[pltpu.VMEM((rows_chip, half), F32)],
        )
        gathered = trade(outgoing).reshape(rows_all, half + SIDE)
        near = call(up_kernel, shape((rows_all + 8, 2 * block + SIDE), F32), gathered, up_pair, bias_rows)
        partial = call(
            functools.partial(down_kernel, step),
            shape((rows_all, half), BF16),
            near, swap(near), active, down_pair,
            specs=[VMEM, VMEM, SMEM, VMEM],
        )
        received = trade(partial.reshape(CHIPS, rows_chip, half))
        done = call(sum_kernel, shape((rows_chip, half), BF16), received, rows, down_bias)
        produced.append(done)
        if step + 1 < TICKS:
            moved = lax.ppermute(done, "pipe", [(i, i + 1) for i in range(pipes - 1)])
    theirs = call(lambda *refs: gather_far_kernel(refs[:-1], refs[-1]), shape((TICKS, rows_dev, half), BF16), *produced)
    return call(
        lambda *refs: final_kernel(refs[:-2], refs[-2], refs[-1]),
        shape((1, TICKS, rows_dev, width), BF16),
        *produced, swap(theirs),
    )


def solution(mesh):
    return jax.shard_map(
        on_device,
        mesh=mesh,
        in_specs=(
            P("pipe", "blk", None),
            P(None, "blk", None),
            P("pipe", None),
            P("pipe", None),
            P("pipe", None, "blk"),
            P("pipe", "blk"),
            P("pipe", "blk", None),
            P("pipe", None),
            P(None, "pipe", None, None),
        ),
        out_specs=P("pipe", None, "blk", None),
        check_vma=False,
    )
```

```python
import functools

import jax
import jax.numpy as jnp
from jax import lax
from jax.experimental import pallas as pl
from jax.experimental.pallas import tpu as pltpu
from jax.sharding import PartitionSpec as P

F32, BF16 = jnp.float32, jnp.bfloat16
TICKS = 4
CHIPS = 16
EPS = 1e-05

VMEM = pl.BlockSpec(memory_space=pltpu.VMEM)
SMEM = pl.BlockSpec(memory_space=pltpu.SMEM)
PARAMS = pltpu.CompilerParams(vmem_limit_bytes=40 * 1024 * 1024)


def is_first(shape):
    return lax.broadcasted_iota(jnp.int32, shape, 0) % 8 < 4


def halves(row_ref, half):
    row = row_ref[...].astype(F32)
    return jnp.where(is_first((8, half)), row[:, :half], row[:, half:])


def row_sum(x):
    part = jnp.broadcast_to(jnp.sum(x, axis=1, keepdims=True), (8, 128))
    return (part + pltpu.roll(part, 4, 0))[:, :1]


def arrange_kernel(stream_ref, arrivals_ref, out_ref, scratch):
    half = out_ref.shape[2]
    for item in range(TICKS):
        rows = (stream_ref[0] if item == 0 else arrivals_ref[item - 1]).astype(F32)
        scratch[item, 0:4] = rows[:, :half]
        scratch[item, 4:8] = rows[:, half:]
        out_ref[item] = scratch[item].astype(BF16)


def norm_kernel(step, moved_ref, local_ref, gain_ref, bias_ref, rows_out, send_out):
    half = rows_out.shape[1]
    rows = local_ref[step].astype(F32)
    if step:
        first = jnp.broadcast_to(lax.axis_index("pipe") == 0, rows.shape)
        rows = jnp.where(first, rows, moved_ref[...].astype(F32))
    rows_out[...] = rows.astype(BF16)
    centred = rows - row_sum(rows) * (0.5 / half)
    var = row_sum(centred * centred) * (0.5 / half)
    scaled = centred * lax.rsqrt(var + EPS)
    normed = (scaled * halves(gain_ref, half) + halves(bias_ref, half)).astype(BF16)
    for chip in range(CHIPS):
        send_out[chip] = normed


def ffn_kernel(step, rows_ref, up_near, up_far, bias_near, bias_far, active_ref, down_near, down_far, out_ref):
    count, half = rows_ref.shape
    block = up_near.shape[2]
    chunk = 512
    j = lax.axis_index("blk")
    tile = j % 2

    def up(at):
        return jnp.concatenate([up_near[0, at : at + chunk], up_far[0, at : at + chunk]], axis=1)

    def down(at):
        return jnp.concatenate([down_near[0, :, at : at + chunk], down_far[0, :, at : at + chunk]], axis=0)

    first = jnp.zeros((count, 2 * block), F32)
    second = jnp.zeros((count, 2 * block), F32)
    for at in range(0, half, chunk):
        rows = rows_ref[:, at : at + chunk]
        first += jnp.dot(rows, up(at), preferred_element_type=F32)
        second += jnp.dot(rows, up(half + at), preferred_element_type=F32)
    low = is_first(first.shape)
    own = jnp.where(low, first, second)
    preact = own + jnp.where(low, pltpu.roll(own, count - 4, 0), pltpu.roll(own, 4, 0))
    flags = []
    for owner in (j, j + 1 - 2 * tile):
        found = jnp.int32(0)
        for k in range(active_ref.shape[3]):
            found = found | (active_ref[step, 0, tile, k] == owner).astype(jnp.int32)
        flags.append(jnp.broadcast_to(found.astype(F32), (1, block)))
    flag = jnp.concatenate(flags, axis=1)
    bias = jnp.concatenate([bias_near[...], bias_far[...]], axis=1).astype(F32)
    acts = (jnp.maximum(preact + bias, 0.0) * flag).astype(BF16)
    low = is_first((count, chunk))
    for at in range(0, half, chunk):
        one = jnp.dot(acts, down(at), preferred_element_type=F32)
        two = jnp.dot(acts, down(half + at), preferred_element_type=F32)
        out_ref[:, at : at + chunk] = jnp.where(low, one, two).astype(BF16)


def sum_kernel(parts_ref, rows_ref, bias_ref, *refs):
    before, out_ref = refs[:-1], refs[-1]
    half = rows_ref.shape[1]
    total = rows_ref[...].astype(F32) + halves(bias_ref, half)
    for chip in range(CHIPS):
        total += parts_ref[chip].astype(F32)
    if before:
        for step, ref in enumerate(before):
            out_ref[step] = ref[...]
        out_ref[len(before)] = total.astype(BF16)
    else:
        out_ref[...] = total.astype(BF16)


def final_kernel(rows_ref, out_ref):
    half = rows_ref.shape[2]
    for step in range(TICKS):
        rows = rows_ref[step].astype(F32)
        out_ref[0, step, :, :half] = rows[0:4].astype(BF16)
        out_ref[0, step, :, half:] = rows[4:8].astype(BF16)


def call(kernel, outs, *args, specs=None, scratch=()):
    single = isinstance(outs, jax.ShapeDtypeStruct)
    return pl.pallas_call(
        kernel,
        out_shape=outs,
        in_specs=list(specs) if specs else [VMEM] * len(args),
        out_specs=VMEM if single else [VMEM] * len(outs),
        scratch_shapes=list(scratch),
        compiler_params=PARAMS,
    )(*args)


def on_device(stream, arrivals, ln_gain, ln_bias, up_weight, up_bias, down_weight, down_bias, active):
    shape = jax.ShapeDtypeStruct
    blocks = lax.axis_size("blk")
    pipes = lax.axis_size("pipe")
    rows_dev, width = stream.shape[1], stream.shape[2]
    half = width // 2
    rows_half = 2 * rows_dev
    same_core = [[2 * chip + core for chip in range(CHIPS)] for core in range(2)]
    homes = [(j, 2 * (j % CHIPS) + j // CHIPS) for j in range(blocks)]

    def swap(x):
        return lax.ppermute(x, "blk", [(i, i ^ 1) for i in range(blocks)])

    def trade(x):
        return lax.all_to_all(x, "blk", 0, 0, axis_index_groups=same_core, tiled=True)

    arranged = call(
        arrange_kernel,
        shape((TICKS, rows_half, half), BF16),
        stream, arrivals,
        scratch=[pltpu.VMEM((TICKS, rows_half, half), F32)],
    )
    local = lax.ppermute(arranged, "blk", homes)
    moved = None
    produced = []
    for step in range(TICKS):
        args = [local, ln_gain, ln_bias] if step == 0 else [moved, local, ln_gain, ln_bias]
        kernel = functools.partial(norm_kernel, step) if step else functools.partial(norm_kernel, 0, None)
        rows, outgoing = call(
            kernel,
            [shape((rows_half, half), BF16), shape((CHIPS, rows_half, half), BF16)],
            *args,
        )
        if step == 0:
            outgoing, *weights = lax.optimization_barrier((outgoing, up_weight, down_weight, up_bias))
            up_far, down_far, bias_far = map(swap, weights)
        gathered = trade(outgoing).reshape(CHIPS * rows_half, half)
        partial = call(
            functools.partial(ffn_kernel, step),
            shape((CHIPS * rows_half, half), BF16),
            gathered, up_weight, up_far, up_bias, bias_far, active, down_weight, down_far,
            specs=[VMEM] * 5 + [SMEM] + [VMEM] * 2,
        )
        received = trade(partial.reshape(CHIPS, rows_half, half))
        if step + 1 < TICKS:
            done = call(sum_kernel, shape((rows_half, half), BF16), received, rows, down_bias)
            produced.append(done)
            moved = lax.ppermute(done, "pipe", [(i, i + 1) for i in range(pipes - 1)])
        else:
            done = call(sum_kernel, shape((TICKS, rows_half, half), BF16), received, rows, down_bias, *produced)
    back = lax.ppermute(done, "blk", [(home, j) for j, home in homes])
    return call(final_kernel, shape((1, TICKS, rows_dev, width), BF16), back)


def solution(mesh):
    return jax.shard_map(
        on_device,
        mesh=mesh,
        in_specs=(
            P("pipe", "blk", None),
            P(None, "blk", None),
            P("pipe", None),
            P("pipe", None),
            P("pipe", None, "blk"),
            P("pipe", "blk"),
            P("pipe", "blk", None),
            P("pipe", None),
            P(None, "pipe", None, None),
        ),
        out_specs=P("pipe", None, "blk", None),
        check_vma=False,
    )
```

```python
import functools

import jax
import jax.numpy as jnp
from jax import lax
from jax.experimental import pallas as pl
from jax.experimental.pallas import tpu as pltpu
from jax.sharding import PartitionSpec as P

F32, BF16 = jnp.float32, jnp.bfloat16
TICKS = 4
CHIPS = 16
EPS = 1e-05

VMEM = pl.BlockSpec(memory_space=pltpu.VMEM)
SMEM = pl.BlockSpec(memory_space=pltpu.SMEM)
COST = pl.CostEstimate(flops=100_000, bytes_accessed=300_000, transcendentals=0)
PARAMS = pltpu.CompilerParams(vmem_limit_bytes=40 * 1024 * 1024)


def is_first(shape):
    return lax.broadcasted_iota(jnp.int32, shape, 0) % 8 < 4


def halves(row_ref, half):
    row = row_ref[...].astype(F32)
    return jnp.where(is_first((8, half)), row[:, :half], row[:, half:])


def row_sum(x):
    part = jnp.broadcast_to(jnp.sum(x, axis=1, keepdims=True), (8, 128))
    return (part + pltpu.roll(part, 4, 0))[:, :1]


def lay_out(rows_ref, scratch, half):
    rows = rows_ref.astype(F32)
    scratch[0:4] = rows[:, :half]
    scratch[4:8] = rows[:, half:]
    return scratch[...].astype(BF16)


def arrange_kernel(stream_ref, arrivals_ref, out_ref, scratch):
    for item in range(out_ref.shape[0]):
        rows = stream_ref[0] if item == 0 else arrivals_ref[item - 1]
        out_ref[item] = lay_out(rows, scratch, out_ref.shape[2])


def halves_kernel(gain, bias, down_bias, gain_out, bias_out, down_bias_out):
    half = gain_out.shape[1]
    gain_out[...] = halves(gain, half)
    bias_out[...] = halves(bias, half)
    down_bias_out[...] = halves(down_bias, half)


def norm_kernel(step, moved_ref, local_ref, gain_ref, bias_ref, rows_out, send_out):
    half = rows_out.shape[1]
    rows = local_ref[step].astype(F32)
    if step:
        first = jnp.broadcast_to(lax.axis_index("pipe") == 0, rows.shape)
        rows = jnp.where(first, rows, moved_ref[...].astype(F32))
    rows_out[...] = rows.astype(BF16)
    centred = rows - row_sum(rows) * (0.5 / half)
    var = row_sum(centred * centred) * (0.5 / half)
    scaled = centred * lax.rsqrt(var + EPS)
    normed = (scaled * gain_ref[...] + bias_ref[...]).astype(BF16)
    for chip in range(CHIPS):
        send_out[chip] = normed


def ffn_kernel(step, rows_ref, up_near, up_far, bias_near, bias_far, active_ref, down_near, down_far, out_ref):
    count, half = rows_ref.shape
    block = up_near.shape[2]
    chunk = 512
    j = lax.axis_index("blk")
    tile = j % 2

    def up(at):
        return jnp.concatenate([up_near[0, at : at + chunk], up_far[0, at : at + chunk]], axis=1)

    def down(at):
        return jnp.concatenate([down_near[0, :, at : at + chunk], down_far[0, :, at : at + chunk]], axis=0)

    first = jnp.zeros((count, 2 * block), F32)
    second = jnp.zeros((count, 2 * block), F32)
    for at in range(0, half, chunk):
        rows = rows_ref[:, at : at + chunk]
        first += jnp.dot(rows, up(at), preferred_element_type=F32)
        second += jnp.dot(rows, up(half + at), preferred_element_type=F32)
    low = is_first(first.shape)
    own = jnp.where(low, first, second)
    preact = own + jnp.where(low, pltpu.roll(own, count - 4, 0), pltpu.roll(own, 4, 0))
    flags = []
    for owner in (j, j + 1 - 2 * tile):
        found = jnp.int32(0)
        for k in range(active_ref.shape[3]):
            found = found | (active_ref[step, 0, tile, k] == owner).astype(jnp.int32)
        flags.append(jnp.broadcast_to(found.astype(F32), (1, block)))
    flag = jnp.concatenate(flags, axis=1)
    bias = jnp.concatenate([bias_near[...], bias_far[...]], axis=1).astype(F32)
    acts = (jnp.maximum(preact + bias, 0.0) * flag).astype(BF16)
    low = is_first((count, chunk))
    for at in range(0, half, chunk):
        one = jnp.dot(acts, down(at), preferred_element_type=F32)
        two = jnp.dot(acts, down(half + at), preferred_element_type=F32)
        out_ref[:, at : at + chunk] = jnp.where(low, one, two).astype(BF16)


def add_up(parts_ref, rows_ref, bias_ref):
    total = rows_ref[...].astype(F32) + bias_ref[...]
    for chip in range(CHIPS):
        total += parts_ref[chip].astype(F32)
    return total.astype(BF16)


def sum_kernel(parts_ref, rows_ref, bias_ref, out_ref):
    out_ref[...] = add_up(parts_ref, rows_ref, bias_ref)


def last_sum_kernel(parts_ref, rows_ref, bias_ref, *refs):
    before, out_ref = refs[:-1], refs[-1]
    for step, ref in enumerate(before):
        out_ref[step] = ref[...]
    out_ref[len(before)] = add_up(parts_ref, rows_ref, bias_ref)


def final_kernel(rows_ref, out_ref):
    half = rows_ref.shape[2]
    for step in range(TICKS):
        rows = rows_ref[step].astype(F32)
        out_ref[0, step, :, :half] = rows[0:4].astype(BF16)
        out_ref[0, step, :, half:] = rows[4:8].astype(BF16)


def home_of(j):
    x, y, core = j // 8, j // 2 % 4, j % 2
    tile = x // 2
    return j if core == tile else 8 * (3 - x) + 2 * y + tile


def call(kernel, outs, *args, specs=None, scratch=(), cost=None):
    single = isinstance(outs, jax.ShapeDtypeStruct)
    return pl.pallas_call(
        kernel,
        out_shape=outs,
        in_specs=list(specs) if specs else [VMEM] * len(args),
        out_specs=VMEM if single else [VMEM] * len(outs),
        scratch_shapes=list(scratch),
        compiler_params=PARAMS,
        cost_estimate=cost,
    )(*args)


def on_device(stream, arrivals, ln_gain, ln_bias, up_weight, up_bias, down_weight, down_bias, active):
    shape = jax.ShapeDtypeStruct
    blocks = lax.axis_size("blk")
    pipes = lax.axis_size("pipe")
    rows_dev, width = stream.shape[1], stream.shape[2]
    half = width // 2
    rows_half = 2 * rows_dev
    same_core = [[2 * chip + core for chip in range(CHIPS)] for core in range(2)]
    homes = [home_of(j) for j in range(blocks)]
    go_home = list(enumerate(homes))

    def swap(x):
        return lax.ppermute(x, "blk", [(i, i ^ 1) for i in range(blocks)])

    def trade(x):
        return lax.all_to_all(x, "blk", 0, 0, axis_index_groups=same_core, tiled=True)

    up_far, down_far = swap(up_weight), swap(down_weight)
    arranged = call(
        arrange_kernel,
        shape((TICKS, rows_half, half), BF16),
        stream, arrivals,
        scratch=[pltpu.VMEM((rows_half, half), F32)],
    )
    local = lax.ppermute(arranged, "blk", go_home)
    gain, bias, bias_down = call(halves_kernel, [shape((rows_half, half), F32)] * 3, ln_gain, ln_bias, down_bias, cost=COST)
    bias_far = swap(up_bias)
    local, bias_far = lax.optimization_barrier((local, bias_far))
    moved = None
    produced = []
    for step in range(TICKS):
        args = [local, gain, bias]
        kernel = functools.partial(norm_kernel, step) if step else functools.partial(norm_kernel, 0, None)
        rows, outgoing = call(
            kernel,
            [shape((rows_half, half), BF16), shape((CHIPS, rows_half, half), BF16)],
            *([moved] if step else []), *args,
        )
        gathered = trade(outgoing).reshape(CHIPS * rows_half, half)
        partial = call(
            functools.partial(ffn_kernel, step),
            shape((CHIPS * rows_half, half), BF16),
            gathered, up_weight, up_far, up_bias, bias_far, active, down_weight, down_far,
            specs=[VMEM] * 5 + [SMEM] + [VMEM] * 2,
        )
        received = trade(partial.reshape(CHIPS, rows_half, half))
        if step + 1 < TICKS:
            done = call(sum_kernel, shape((rows_half, half), BF16), received, rows, bias_down)
            produced.append(done)
            moved = lax.ppermute(done, "pipe", [(i, i + 1) for i in range(pipes - 1)])
        else:
            done = call(last_sum_kernel, shape((TICKS, rows_half, half), BF16), received, rows, bias_down, *produced)
    back = lax.ppermute(done, "blk", [(home, j) for j, home in enumerate(homes)])
    return call(final_kernel, shape((1, TICKS, rows_dev, width), BF16), back)


def solution(mesh):
    return jax.shard_map(
        on_device,
        mesh=mesh,
        in_specs=(
            P("pipe", "blk", None),
            P(None, "blk", None),
            P("pipe", None),
            P("pipe", None),
            P("pipe", None, "blk"),
            P("pipe", "blk"),
            P("pipe", "blk", None),
            P("pipe", None),
            P(None, "pipe", None, None),
        ),
        out_specs=P("pipe", None, "blk", None),
        check_vma=False,
    )
```

```python
import functools

import jax
import jax.numpy as jnp
from jax import lax
from jax.experimental import pallas as pl
from jax.experimental.pallas import tpu as pltpu
from jax.sharding import PartitionSpec as P

F32, BF16 = jnp.float32, jnp.bfloat16
TICKS = 4
CHIPS = 16
EPS = 1e-05

VMEM = pl.BlockSpec(memory_space=pltpu.VMEM)
SMEM = pl.BlockSpec(memory_space=pltpu.SMEM)
COST = pl.CostEstimate(flops=100_000, bytes_accessed=300_000, transcendentals=0)
PARAMS = pltpu.CompilerParams(vmem_limit_bytes=40 * 1024 * 1024)


def is_first(shape):
    return lax.broadcasted_iota(jnp.int32, shape, 0) % 8 < 4


def halves(row_ref, half):
    row = row_ref[...].astype(F32)
    return jnp.where(is_first((8, half)), row[:, :half], row[:, half:])


def row_sum(x):
    part = jnp.broadcast_to(jnp.sum(x, axis=1, keepdims=True), (8, 128))
    return (part + pltpu.roll(part, 4, 0))[:, :1]


def lay_out(rows_ref, scratch, half):
    rows = rows_ref.astype(F32)
    scratch[0:4] = rows[:, :half]
    scratch[4:8] = rows[:, half:]
    return scratch[...].astype(BF16)


def arrange_kernel(stream_ref, arrivals_ref, out_ref, scratch):
    for item in range(out_ref.shape[0]):
        rows = stream_ref[0] if item == 0 else arrivals_ref[item - 1]
        out_ref[item] = lay_out(rows, scratch, out_ref.shape[2])


def halves_kernel(gain, bias, gain_out, bias_out):
    half = gain_out.shape[1]
    gain_out[...] = halves(gain, half)
    bias_out[...] = halves(bias, half)


def norm_kernel(step, moved_ref, local_ref, gain_ref, bias_ref, rows_out, send_out):
    half = rows_out.shape[1]
    rows = local_ref[step].astype(F32)
    if step:
        first = jnp.broadcast_to(lax.axis_index("pipe") == 0, rows.shape)
        rows = jnp.where(first, rows, moved_ref[...].astype(F32))
    rows_out[...] = rows.astype(BF16)
    centred = rows - row_sum(rows) * (0.5 / half)
    var = row_sum(centred * centred) * (0.5 / half)
    scaled = centred * lax.rsqrt(var + EPS)
    normed = (scaled * gain_ref[...] + bias_ref[...]).astype(BF16)
    for chip in range(CHIPS):
        send_out[chip] = normed


def ffn_kernel(step, rows_ref, up_near, up_far, bias_near, bias_far, active_ref, down_near, down_far, out_ref):
    count, half = rows_ref.shape
    block = up_near.shape[2]
    chunk = 512
    j = lax.axis_index("blk")
    tile = j % 2

    def up(at):
        return jnp.concatenate([up_near[0, at : at + chunk], up_far[0, at : at + chunk]], axis=1)

    def down(at):
        return jnp.concatenate([down_near[0, :, at : at + chunk], down_far[0, :, at : at + chunk]], axis=0)

    first = jnp.zeros((count, 2 * block), F32)
    second = jnp.zeros((count, 2 * block), F32)
    for at in range(0, half, chunk):
        rows = rows_ref[:, at : at + chunk]
        first += jnp.dot(rows, up(at), preferred_element_type=F32)
        second += jnp.dot(rows, up(half + at), preferred_element_type=F32)
    low = is_first(first.shape)
    own = jnp.where(low, first, second)
    preact = own + jnp.where(low, pltpu.roll(own, count - 4, 0), pltpu.roll(own, 4, 0))
    flags = []
    for owner in (j, j + 1 - 2 * tile):
        found = jnp.int32(0)
        for k in range(active_ref.shape[3]):
            found = found | (active_ref[step, 0, tile, k] == owner).astype(jnp.int32)
        flags.append(jnp.broadcast_to(found.astype(F32), (1, block)))
    flag = jnp.concatenate(flags, axis=1)
    bias = jnp.concatenate([bias_near[...], bias_far[...]], axis=1).astype(F32)
    acts = (jnp.maximum(preact + bias, 0.0) * flag).astype(BF16)
    low = is_first((count, chunk))
    for at in range(0, half, chunk):
        one = jnp.dot(acts, down(at), preferred_element_type=F32)
        two = jnp.dot(acts, down(half + at), preferred_element_type=F32)
        out_ref[:, at : at + chunk] = jnp.where(low, one, two).astype(BF16)


def add_up(parts_ref, rows_ref, bias_ref):
    total = rows_ref[...].astype(F32) + halves(bias_ref, rows_ref.shape[1])
    for chip in range(CHIPS):
        total += parts_ref[chip].astype(F32)
    return total.astype(BF16)


def sum_kernel(parts_ref, rows_ref, bias_ref, out_ref):
    out_ref[...] = add_up(parts_ref, rows_ref, bias_ref)


def last_sum_kernel(parts_ref, rows_ref, bias_ref, *refs):
    before, out_ref = refs[:-1], refs[-1]
    for step, ref in enumerate(before):
        out_ref[step] = ref[...]
    out_ref[len(before)] = add_up(parts_ref, rows_ref, bias_ref)


def final_kernel(rows_ref, out_ref):
    half = rows_ref.shape[2]
    for step in range(TICKS):
        rows = rows_ref[step].astype(F32)
        out_ref[0, step, :, :half] = rows[0:4].astype(BF16)
        out_ref[0, step, :, half:] = rows[4:8].astype(BF16)


def home_of(j):
    x, y, core = j // 8, j // 2 % 4, j % 2
    tile = x // 2
    return j if core == tile else 8 * (3 - x) + 2 * y + tile


def call(kernel, outs, *args, specs=None, scratch=(), cost=None):
    single = isinstance(outs, jax.ShapeDtypeStruct)
    return pl.pallas_call(
        kernel,
        out_shape=outs,
        in_specs=list(specs) if specs else [VMEM] * len(args),
        out_specs=VMEM if single else [VMEM] * len(outs),
        scratch_shapes=list(scratch),
        compiler_params=PARAMS,
        cost_estimate=cost,
    )(*args)


def on_device(stream, arrivals, ln_gain, ln_bias, up_weight, up_bias, down_weight, down_bias, active):
    shape = jax.ShapeDtypeStruct
    blocks = lax.axis_size("blk")
    pipes = lax.axis_size("pipe")
    rows_dev, width = stream.shape[1], stream.shape[2]
    half = width // 2
    rows_half = 2 * rows_dev
    by_core = (lambda k: 8 * (k % 4) + 2 * (k // 4), lambda k: 2 * k + 1)
    same_core = [[device(k) for k in range(CHIPS)] for device in by_core]
    homes = [home_of(j) for j in range(blocks)]
    go_home = list(enumerate(homes))

    def swap(x):
        return lax.ppermute(x, "blk", [(i, i ^ 1) for i in range(blocks)])

    def trade(x):
        return lax.all_to_all(x, "blk", 0, 0, axis_index_groups=same_core, tiled=True)

    up_far, down_far = swap(up_weight), swap(down_weight)
    arranged = call(
        arrange_kernel,
        shape((TICKS, rows_half, half), BF16),
        stream, arrivals,
        scratch=[pltpu.VMEM((rows_half, half), F32)],
    )
    local = lax.ppermute(arranged, "blk", go_home)
    gain, bias = call(halves_kernel, [shape((rows_half, half), F32)] * 2, ln_gain, ln_bias, cost=COST)
    bias_far = swap(up_bias)
    local, bias_far = lax.optimization_barrier((local, bias_far))
    moved = None
    produced = []
    for step in range(TICKS):
        args = [local, gain, bias]
        kernel = functools.partial(norm_kernel, step) if step else functools.partial(norm_kernel, 0, None)
        rows, outgoing = call(
            kernel,
            [shape((rows_half, half), BF16), shape((CHIPS, rows_half, half), BF16)],
            *([moved] if step else []), *args,
        )
        gathered = trade(outgoing).reshape(CHIPS * rows_half, half)
        partial = call(
            functools.partial(ffn_kernel, step),
            shape((CHIPS * rows_half, half), BF16),
            gathered, up_weight, up_far, up_bias, bias_far, active, down_weight, down_far,
            specs=[VMEM] * 5 + [SMEM] + [VMEM] * 2,
        )
        received = trade(partial.reshape(CHIPS, rows_half, half))
        if step + 1 < TICKS:
            done = call(sum_kernel, shape((rows_half, half), BF16), received, rows, down_bias)
            produced.append(done)
            moved = lax.ppermute(done, "pipe", [(i, i + 1) for i in range(pipes - 1)])
        else:
            done = call(last_sum_kernel, shape((TICKS, rows_half, half), BF16), received, rows, down_bias, *produced)
    back = lax.ppermute(done, "blk", [(home, j) for j, home in enumerate(homes)])
    return call(final_kernel, shape((1, TICKS, rows_dev, width), BF16), back)


def solution(mesh):
    return jax.shard_map(
        on_device,
        mesh=mesh,
        in_specs=(
            P("pipe", "blk", None),
            P(None, "blk", None),
            P("pipe", None),
            P("pipe", None),
            P("pipe", None, "blk"),
            P("pipe", "blk"),
            P("pipe", "blk", None),
            P("pipe", None),
            P(None, "pipe", None, None),
        ),
        out_specs=P("pipe", None, "blk", None),
        check_vma=False,
    )
```

```python
import functools

import jax
import jax.numpy as jnp
from jax import lax
from jax.experimental import pallas as pl
from jax.experimental.pallas import tpu as pltpu
from jax.sharding import PartitionSpec as P

F32, BF16 = jnp.float32, jnp.bfloat16
TICKS = 4
CHIPS = 16
EPS = 1e-05

VMEM = pl.BlockSpec(memory_space=pltpu.VMEM)
SMEM = pl.BlockSpec(memory_space=pltpu.SMEM)
COST = pl.CostEstimate(flops=100_000, bytes_accessed=300_000, transcendentals=0)
PARAMS = pltpu.CompilerParams(vmem_limit_bytes=16 * 1024 * 1024)


def is_first(shape):
    return lax.broadcasted_iota(jnp.int32, shape, 0) % 8 < 4


def halves(row_ref, half):
    row = row_ref[...].astype(F32)
    return jnp.where(is_first((8, half)), row[:, :half], row[:, half:])


def row_sum(x):
    part = jnp.broadcast_to(jnp.sum(x, axis=1, keepdims=True), (8, 128))
    return (part + pltpu.roll(part, 4, 0))[:, :1]


def lay_out(rows_ref, scratch, half):
    rows = rows_ref.astype(F32)
    scratch[0:4] = rows[:, :half]
    scratch[4:8] = rows[:, half:]
    return scratch[...].astype(BF16)


def arrange_kernel(stream_ref, arrivals_ref, out_ref, scratch):
    for item in range(out_ref.shape[0]):
        rows = stream_ref[0] if item == 0 else arrivals_ref[item - 1]
        out_ref[item] = lay_out(rows, scratch, out_ref.shape[2])


def halves_kernel(gain, bias, gain_out, bias_out):
    half = gain_out.shape[1]
    gain_out[...] = halves(gain, half)
    bias_out[...] = halves(bias, half)


def norm_kernel(step, moved_ref, local_ref, gain_ref, bias_ref, rows_out, send_out):
    half = rows_out.shape[1]
    rows = local_ref[step].astype(F32)
    if step:
        first = jnp.broadcast_to(lax.axis_index("pipe") == 0, rows.shape)
        rows = jnp.where(first, rows, moved_ref[...].astype(F32))
    rows_out[...] = rows.astype(BF16)
    centred = rows - row_sum(rows) * (0.5 / half)
    var = row_sum(centred * centred) * (0.5 / half)
    scaled = centred * lax.rsqrt(var + EPS)
    normed = (scaled * gain_ref[...] + bias_ref[...]).astype(BF16)
    for chip in range(CHIPS):
        send_out[chip] = normed


def ffn_kernel(step, rows_ref, up_near, up_far, bias_near, active_ref, down_near, down_far, out_ref):
    count, half = rows_ref.shape
    block = up_near.shape[2]
    bias_far = up_far[0, 2 * half : 2 * half + 16, :].astype(F32)[:1]
    chunk = 1024
    j = lax.axis_index("blk")
    tile = j % 2

    def up(at):
        return jnp.concatenate([up_near[0, at : at + chunk], up_far[0, at : at + chunk]], axis=1)

    def down(at):
        return jnp.concatenate([down_near[0, :, at : at + chunk], down_far[0, :, at : at + chunk]], axis=0)

    first = jnp.zeros((count, 2 * block), F32)
    second = jnp.zeros((count, 2 * block), F32)
    for at in range(0, half, chunk):
        rows = rows_ref[:, at : at + chunk]
        first += jnp.dot(rows, up(at), preferred_element_type=F32)
        second += jnp.dot(rows, up(half + at), preferred_element_type=F32)
    low = is_first(first.shape)
    own = jnp.where(low, first, second)
    preact = own + jnp.where(low, pltpu.roll(own, count - 4, 0), pltpu.roll(own, 4, 0))
    flags = []
    for owner in (j, j + 1 - 2 * tile):
        found = jnp.int32(0)
        for k in range(active_ref.shape[3]):
            found = found | (active_ref[step, 0, tile, k] == owner).astype(jnp.int32)
        flags.append(jnp.broadcast_to(found.astype(F32), (1, block)))
    flag = jnp.concatenate(flags, axis=1)
    bias = jnp.concatenate([bias_near[...].astype(F32), bias_far], axis=1)
    acts = (jnp.maximum(preact + bias, 0.0) * flag).astype(BF16)
    low = is_first((count, chunk))
    for at in range(0, half, chunk):
        one = jnp.dot(acts, down(at), preferred_element_type=F32)
        two = jnp.dot(acts, down(half + at), preferred_element_type=F32)
        out_ref[:, at : at + chunk] = jnp.where(low, one, two).astype(BF16)


def add_up(parts_ref, rows_ref, bias_ref):
    total = rows_ref[...].astype(F32) + halves(bias_ref, rows_ref.shape[1])
    for chip in range(CHIPS):
        total += parts_ref[chip].astype(F32)
    return total.astype(BF16)


def sum_kernel(parts_ref, rows_ref, bias_ref, out_ref):
    out_ref[...] = add_up(parts_ref, rows_ref, bias_ref)


def last_sum_kernel(parts_ref, rows_ref, bias_ref, *refs):
    before, out_ref = refs[:-1], refs[-1]
    for step, ref in enumerate(before):
        out_ref[step] = ref[...]
    out_ref[len(before)] = add_up(parts_ref, rows_ref, bias_ref)


def final_kernel(rows_ref, out_ref):
    half = rows_ref.shape[2]
    for step in range(TICKS):
        rows = rows_ref[step].astype(F32)
        out_ref[0, step, :, :half] = rows[0:4].astype(BF16)
        out_ref[0, step, :, half:] = rows[4:8].astype(BF16)


def home_of(j):
    x, y, core = j // 8, j // 2 % 4, j % 2
    tile = x // 2
    return j if core == tile else 8 * (3 - x) + 2 * y + tile


def call(kernel, outs, *args, specs=None, scratch=(), cost=None):
    single = isinstance(outs, jax.ShapeDtypeStruct)
    return pl.pallas_call(
        kernel,
        out_shape=outs,
        in_specs=list(specs) if specs else [VMEM] * len(args),
        out_specs=VMEM if single else [VMEM] * len(outs),
        scratch_shapes=list(scratch),
        compiler_params=PARAMS,
        cost_estimate=cost,
    )(*args)


def on_device(stream, arrivals, ln_gain, ln_bias, up_weight, up_bias, down_weight, down_bias, active):
    shape = jax.ShapeDtypeStruct
    blocks = lax.axis_size("blk")
    pipes = lax.axis_size("pipe")
    rows_dev, width = stream.shape[1], stream.shape[2]
    half = width // 2
    rows_half = 2 * rows_dev
    by_core = (lambda k: 8 * (k % 4) + 2 * (k // 4), lambda k: 2 * k + 1)
    same_core = [[device(k) for k in range(CHIPS)] for device in by_core]
    homes = [home_of(j) for j in range(blocks)]
    go_home = list(enumerate(homes))

    def swap(x):
        return lax.ppermute(x, "blk", [(i, i ^ 1) for i in range(blocks)])

    def trade(x):
        return lax.all_to_all(x, "blk", 0, 0, axis_index_groups=same_core, tiled=True)

    below = jnp.pad(up_bias[:, None], ((0, 0), (0, 15), (0, 0)))
    up_far, down_far = swap(jnp.concatenate([up_weight, below], axis=1)), swap(down_weight)
    arranged = call(
        arrange_kernel,
        shape((TICKS, rows_half, half), BF16),
        stream, arrivals,
        scratch=[pltpu.VMEM((rows_half, half), F32)],
    )
    local = lax.ppermute(arranged, "blk", go_home)
    gain, bias = call(halves_kernel, [shape((rows_half, half), F32)] * 2, ln_gain, ln_bias, cost=COST)
    moved = None
    produced = []
    for step in range(TICKS):
        args = [local, gain, bias]
        kernel = functools.partial(norm_kernel, step) if step else functools.partial(norm_kernel, 0, None)
        rows, outgoing = call(
            kernel,
            [shape((rows_half, half), BF16), shape((CHIPS, rows_half, half), BF16)],
            *([moved] if step else []), *args,
        )
        gathered = trade(outgoing).reshape(CHIPS * rows_half, half)
        partial = call(
            functools.partial(ffn_kernel, step),
            shape((CHIPS * rows_half, half), BF16),
            gathered, up_weight, up_far, up_bias, active, down_weight, down_far,
            specs=[VMEM] * 4 + [SMEM] + [VMEM] * 2,
        )
        received = trade(partial.reshape(CHIPS, rows_half, half))
        if step + 1 < TICKS:
            done = call(sum_kernel, shape((rows_half, half), BF16), received, rows, down_bias)
            produced.append(done)
            moved = lax.ppermute(done, "pipe", [(i, i + 1) for i in range(pipes - 1)])
        else:
            done = call(last_sum_kernel, shape((TICKS, rows_half, half), BF16), received, rows, down_bias, *produced)
    back = lax.ppermute(done, "blk", [(home, j) for j, home in enumerate(homes)])
    return call(final_kernel, shape((1, TICKS, rows_dev, width), BF16), back)


def solution(mesh):
    return jax.shard_map(
        on_device,
        mesh=mesh,
        in_specs=(
            P("pipe", "blk", None),
            P(None, "blk", None),
            P("pipe", None),
            P("pipe", None),
            P("pipe", None, "blk"),
            P("pipe", "blk"),
            P("pipe", "blk", None),
            P("pipe", None),
            P(None, "pipe", None, None),
        ),
        out_specs=P("pipe", None, "blk", None),
        check_vma=False,
    )
```
